32 devices in a mesh: sect: 4 (over y, x), blk: 8 (over z, core).
Axes of the slice: x: 2, y: 2, z: 4, core: 2. Of those that a mesh axis runs over, the one named last changes fastest.
Arguments:
- queries: bfloat16 [1024, 4096], P('blk', 'sect'), may hold values from -512 to 512
- kv_cache: bfloat16 [1024, 32, 2048], P('blk', None, 'sect'), may hold values from -6 to 6
- lengths: int32 [1024], P('blk'), may hold values from 1 to 32, 16384 in all
- resid_in: bfloat16 [1024, 4096], P('blk', 'sect'), may hold values from -10 to 10
- norm_gain: float32 [4096], replicated, may hold values from 0.1 to 1.9
- w_gate: bfloat16 [4096, 14336], P(None, 'blk'), may hold values from -0.09375 to 0.09375
- w_up: bfloat16 [4096, 14336], P(None, 'blk'), may hold values from -0.09375 to 0.09375
- w_down: bfloat16 [14336, 4096], P('blk'), may hold values from -0.046875 to 0.046875
Outputs:
- layer_out: bfloat16 [1024, 4096], P('blk', 'sect')
The draws below stay inside these ranges and needn't reach their ends.
Inputs may be any that keep to these rules, and one draw needn't show every extreme that they name: `lengths`: each row has 1 to 32 live slots and some row has exactly 32.
All inputs are finite; a program needn't handle non-finite values. No bound on the sum of `lengths` on one device may be relied on, other than what follows from the above.
Results may differ from the reference program's by a relative error of at most 0.0068.
Values may be sent and summed in bfloat16 or wider, within the bound.
A program may use at most 128 MiB of HBM per device.

```python
import math
import jax
import jax.numpy as jnp
import numpy as np
from jax import lax

HD = 128
HQ = 32
KVH = 8
D = 4096
FF = 14336
L_MAX = 32
GROUP = 4
ROWS = 1024


def front_slots(key):
    base = jax.random.normal(jax.random.fold_in(key, 7), (ROWS, 2, KVH, 2, HD), jnp.float32)
    base = jnp.clip(base, -6.0, 6.0)
    return base


def draw_kv_cache(key, part):
    front = front_slots(key)
    rest = jax.random.normal(jax.random.fold_in(key, 8), (ROWS, L_MAX - 2, KVH, 2, HD), jnp.float32)
    rest = jnp.clip(rest, -6.0, 6.0)
    whole = jnp.concatenate([front, rest], axis=1)
    return whole.reshape(ROWS, L_MAX, KVH * 2 * HD).astype(jnp.bfloat16)


def draw_queries(key, part):
    drawn = jax.random.normal(jax.random.fold_in(key, 11), (ROWS, KVH, GROUP, HD), jnp.float32)
    drawn = jnp.clip(drawn, -6.0, 6.0)
    return drawn.reshape(ROWS, HQ * HD).astype(jnp.bfloat16)


def draw_resid_in(key, part):
    column = jnp.arange(D, dtype=jnp.float32) / D
    values = jnp.clip(jax.random.normal(jax.random.fold_in(key, 21), (ROWS, D), jnp.float32), -4.0, 4.0)
    trend = 3.0 ** (column - 0.5)
    rowscale = jnp.exp(jax.random.uniform(jax.random.fold_in(key, 22), (ROWS, 1), jnp.float32, jnp.log(0.1), 0.0))
    colnoise = jnp.exp(jax.random.uniform(jax.random.fold_in(key, 23), (1, D), jnp.float32, -0.35, 0.35))
    return (values * rowscale * trend[None, :] * colnoise).astype(jnp.bfloat16)


def block_levels(key, dims, pieces, low, largest):
    def one(dim, parts):
        heights = jax.random.uniform(jax.random.fold_in(jax.random.fold_in(key, 6), dim), (parts,), jnp.float32, low / len(pieces), largest / len(pieces))
        return jnp.repeat(jnp.exp(heights), dims[dim] // parts).reshape((-1,) + (1,) * (len(dims) - dim - 1))

    factor_of = one(*pieces[0])
    for cut in pieces[1:]:
        factor_of = factor_of * one(*cut)
    return factor_of


def profile(amount, total, reach, lean):
    weights = [(1 << 20) // math.isqrt(grade ** lean) + 1 for grade in range(2, amount + 1)]
    spare, holding = total - reach - (amount - 1), [1] * (amount - 1)
    while spare > 0:
        free = [i for i in range(amount - 1) if holding[i] < reach]
        pool, remaining = sum([weights[i] for i in free]), spare
        for i in free:
            more = min(reach - holding[i], max(1, remaining * weights[i] // pool), spare)
            holding[i] = holding[i] + more
            spare = spare - more
    return np.array([reach] + holding)


def uneven(rng, amount, total, most, slope):
    if amount == 2:
        one = jax.random.randint(rng, (), max(1, total - most), min(most, total - 1) + 1)
        return jnp.stack([one, total - one])
    tallies = jnp.asarray(profile(amount, total, most, slope), jnp.int32)
    couples = (amount - 1) // 2
    source_of, receiver = tallies[1:1 + 2 * couples:2], tallies[2:2 + 2 * couples:2]
    room = jnp.minimum(source_of - 1, most - receiver)
    shifted = jax.random.randint(jax.random.fold_in(rng, 1), (couples,), 0, 1 << 20) % (room + 1)
    tallies = tallies.at[1:1 + 2 * couples:2].set(source_of - shifted).at[2:2 + 2 * couples:2].set(receiver + shifted)
    return tallies[jax.random.permutation(jax.random.fold_in(rng, 2), amount)]


def bell_draw(own_key, shape, deviation, limit, pieces=(), kind=jnp.bfloat16):
    array = deviation * jax.random.normal(own_key, shape, jnp.float32)
    if pieces:
        array = array * block_levels(own_key, shape, pieces, -0.22, 0.18)
    return jnp.clip(array, -limit, limit).astype(kind)


def setup_inputs(seed: int = 0) -> dict:
    key_list = jax.random.split(jax.random.key(seed), 9)
    queries = draw_queries(jax.random.fold_in(key_list[8], 71), 0)
    kv_cache = draw_kv_cache(jax.random.fold_in(key_list[8], 71), 0)
    lengths = uneven(key_list[2], ROWS, ROWS * L_MAX // 2, L_MAX, 2).astype(jnp.int32)
    resid_in = draw_resid_in(jax.random.fold_in(key_list[8], 71), 0)
    norm_gain = jnp.clip(1.0 + 0.18 * jax.random.normal(key_list[4], (D,), jnp.float32), 0.1, 1.9)
    w_gate = bell_draw(key_list[5], (D, FF), D ** -0.5, 0.09375, ((1, 8),))
    w_up = bell_draw(key_list[6], (D, FF), D ** -0.5, 0.09375, ((1, 8),))
    w_down = bell_draw(key_list[7], (FF, D), FF ** -0.5, 0.046875, ((0, 8),))
    return dict(queries=queries, kv_cache=kv_cache, lengths=lengths, resid_in=resid_in, norm_gain=norm_gain, w_gate=w_gate, w_up=w_up, w_down=w_down)


def reference(queries, kv_cache, lengths, resid_in, norm_gain, w_gate, w_up, w_down):
    query = queries.astype(jnp.float32).reshape(ROWS, KVH, GROUP, HD)
    cache = kv_cache.astype(jnp.float32).reshape(ROWS, L_MAX, KVH, 2, HD)
    keys = cache[:, :, :, 0, :]
    values = cache[:, :, :, 1, :]
    scores = jnp.einsum('rkgd,rlkd->rkgl', query, keys) / jnp.sqrt(jnp.float32(HD))
    slots = jnp.arange(L_MAX, dtype=jnp.int32)
    live = slots[None, None, None, :] < lengths[:, None, None, None]
    scores = jnp.where(live, scores, jnp.float32(-1e+30))
    top = lax.optimization_barrier(jnp.max(scores, axis=-1, keepdims=True))
    expo = jnp.where(live, jnp.exp(scores - top), jnp.float32(0.0))
    probs = (expo / lax.optimization_barrier(jnp.sum(expo, axis=-1, keepdims=True))).astype(jnp.bfloat16)
    attn = jnp.einsum('rkgl,rlkd->rkgd', probs.astype(jnp.float32), values).reshape(ROWS, D)
    hidden_state = (resid_in.astype(jnp.float32) + attn).astype(jnp.bfloat16)
    state = hidden_state.astype(jnp.float32)
    meansq = lax.optimization_barrier(jnp.mean(state * state, axis=1, keepdims=True))
    normed = (state * lax.rsqrt(meansq + 1e-05) * norm_gain[None, :]).astype(jnp.bfloat16)
    gate = jnp.dot(normed, w_gate, preferred_element_type=jnp.float32)
    upval = jnp.dot(normed, w_up, preferred_element_type=jnp.float32)
    act = (jax.nn.silu(gate) * upval).astype(jnp.bfloat16)
    ffn_out = jnp.dot(act, w_down, preferred_element_type=jnp.float32)
    return (state + ffn_out).astype(jnp.bfloat16)
```

```python
import functools

import jax
import jax.numpy as jnp
from jax import lax
from jax.experimental import pallas as pl
from jax.experimental.pallas import tpu as pltpu
from jax.sharding import PartitionSpec as P

HD = 128
GROUP = 4
TILE = 16
MESH = pl.DeviceIdType.MESH
F32 = jnp.float32
BF16 = jnp.bfloat16


def kernel(
    S, C,
    q_ref, kv_hbm, len_ref, resid_ref, gain_ref, wg_hbm, wu_hbm, wd_hbm,
    out_ref,
    wg, wu, wd, hb, rs, xs, ss, sr, sb, ru, rd, own, fo, ob,
    kv_sem, w_sem, a_send, a_recv, x_send, x_recv, s_send, s_recv,
    l_send, u_recv, d_recv, o_send, o_recv,
):
    RS = rs.shape[1]
    KC = rs.shape[2]
    B = 2 * C
    FFL = wg.shape[2]
    heads = kv_hbm.shape[2] // (2 * HD)
    slots = kv_hbm.shape[1]
    NT = 256 if FFL % 256 == 0 else 128
    NK = 256 if KC % 256 == 0 else 128

    sect = lax.axis_index("sect")
    blk = lax.axis_index("blk")
    chip = blk // 2
    core = blk % 2
    sib = chip * 2 + (1 - core)
    up = blk + 2
    down = blk - 2
    has_up = chip < C - 1
    has_down = chip > 0
    me = core * C + chip

    def order(i):
        return lax.rem(sect + 1 + i, S)

    def remote(src, dst, ssem, rsem, dev):
        return pltpu.make_async_remote_copy(
            src_ref=src, dst_ref=dst, send_sem=ssem, recv_sem=rsem,
            device_id=dev, device_id_type=MESH,
        )

    def weight_copy(i, w):
        t = order(i)
        rows = pl.ds(pl.multiple_of(t * KC, KC), KC)
        src = (wg_hbm.at[rows, :], wu_hbm.at[rows, :], wd_hbm.at[:, rows])[w]
        return pltpu.make_async_copy(src, (wg, wu, wd)[w].at[t], w_sem.at[w, t])

    def greet():
        barrier = pltpu.get_barrier_semaphore()
        for e in range(1, S):
            pl.semaphore_signal(
                barrier, inc=1, device_id={"sect": lax.rem(sect + e, S)}, device_id_type=MESH
            )
        pl.semaphore_signal(barrier, inc=1, device_id={"blk": sib}, device_id_type=MESH)

        @pl.when(has_up)
        def _():
            pl.semaphore_signal(barrier, inc=1, device_id={"blk": up}, device_id_type=MESH)

        @pl.when(has_down)
        def _():
            pl.semaphore_signal(barrier, inc=1, device_id={"blk": down}, device_id_type=MESH)

        pl.semaphore_wait(barrier, S + has_up.astype(jnp.int32) + has_down.astype(jnp.int32))

    def a_copy(t):
        return remote(hb.at[t], rs.at[sect], a_send.at[t], a_recv.at[sect], {"sect": t})

    def a_wait(t):
        remote(hb.at[t], rs.at[t], a_send.at[t], a_recv.at[t], {"sect": t}).wait_recv()

    def front(kv):
        def kv_copy(t):
            rows = pl.ds(pl.multiple_of(t * RS, RS), RS)
            return pltpu.make_async_copy(kv_hbm.at[rows], kv.at[t], kv_sem.at[t])

        for i in range(S):
            kv_copy(order(i)).start()
        for i in range(S):
            weight_copy(i, 0).start()
            weight_copy(i, 1).start()
        for i in range(S):
            weight_copy(i, 2).start()

        def attend(t, dst, slot):
            kv_copy(t).wait()
            for g in range(RS // TILE):
                rows = pl.ds(pl.multiple_of(t * RS + g * TILE, TILE), TILE)
                count = jnp.concatenate([len_ref[rows, :]] * GROUP, axis=0)
                shape = (GROUP * TILE, TILE * slots)
                row = lax.rem(lax.broadcasted_iota(jnp.int32, shape, 0), TILE)
                col = lax.broadcasted_iota(jnp.int32, shape, 1) - row * slots
                live = (col >= 0) & (col < count)
                for h in range(heads):
                    base = h * GROUP * HD
                    query = jnp.concatenate(
                        [q_ref[rows, base + e * HD:base + (e + 1) * HD] for e in range(GROUP)], axis=0
                    )
                    part = kv[t, g * TILE:(g + 1) * TILE, :, h * 2 * HD:(h + 1) * 2 * HD]
                    part = part.reshape(TILE * slots, 2 * HD)
                    scores = lax.dot_general(
                        query, part[:, :HD], (((1,), (1,)), ((), ())), preferred_element_type=F32
                    ) * (HD ** -0.5)
                    scores = jnp.where(live, scores, -1e30)
                    top = jnp.max(scores, axis=1, keepdims=True)
                    expo = jnp.where(live, jnp.exp(scores - top), 0.0)
                    probs = (expo / jnp.sum(expo, axis=1, keepdims=True)).astype(BF16)
                    attn = jnp.dot(probs, part[:, HD:], preferred_element_type=F32)
                    for e in range(GROUP):
                        cols = slice(base + e * HD, base + (e + 1) * HD)
                        dst[slot, g * TILE:(g + 1) * TILE, cols] = (
                            resid_ref[rows, cols].astype(F32) + attn[e * TILE:(e + 1) * TILE]
                        ).astype(BF16)

        greet()

        @pl.loop(0, S - 1)
        def _(i):
            t = order(i)
            attend(t, hb, t)
            a_copy(t).start()

        attend(sect, rs, sect)

    pl.run_scoped(front, pltpu.VMEM((S, RS, slots, kv_hbm.shape[2]), BF16))

    def x_line(j, c, which):
        slot = core * C + c
        return remote(
            xs.at[j, slot], xs.at[j, slot], x_send.at[j, c, which], x_recv.at[j, slot],
            {"blk": up if which == 0 else down},
        )

    def x_sib(j, c):
        slot = core * C + c
        return remote(
            xs.at[j, slot], xs.at[j, slot], x_send.at[j, c, 2], x_recv.at[j, slot], {"blk": sib}
        )

    def x_wait(j, slot):
        remote(
            xs.at[j, slot], xs.at[j, slot], x_send.at[j, 0, 0], x_recv.at[j, slot], {"blk": sib}
        ).wait_recv()

    def send_own(j):
        @pl.when(has_up)
        def _():
            x_line(j, chip, 0).start()

        @pl.when(has_down)
        def _():
            x_line(j, chip, 1).start()

        x_sib(j, chip).start()

    def pass_on(j):
        for s in range(1, C):
            @pl.when(chip - s >= 0)
            def _():
                x_wait(j, core * C + chip - s)

                @pl.when(has_up)
                def _():
                    x_line(j, chip - s, 0).start()

                x_sib(j, chip - s).start()

            @pl.when(chip + s < C)
            def _():
                x_wait(j, core * C + chip + s)

                @pl.when(has_down)
                def _():
                    x_line(j, chip + s, 1).start()

                x_sib(j, chip + s).start()

    def middle(acc_g, acc_u, act, pf):
        acc_g[...] = jnp.zeros_like(acc_g)
        acc_u[...] = jnp.zeros_like(acc_u)

        square = jnp.zeros((RS, 1), F32)
        for i in range(S - 1):
            a_wait(lax.rem(sect + 1 + i, S))
        for t in range(S):
            state = rs[t].astype(F32)
            square = square + jnp.sum(state * state, axis=1, keepdims=True)
        inv = lax.rsqrt(square / (S * KC) + 1e-5)
        for i in range(S):
            t = order(i)
            xs[t, me] = (rs[t].astype(F32) * inv * gain_ref[t]).astype(BF16)
            if i < 2:
                send_own(t)

        @pl.loop(0, S)
        def _(i):
            j = order(i)
            pass_on(j)

            @pl.when(i + 2 < S)
            def _():
                send_own(order(i + 2))

            for c in range(C):
                x_wait(j, (1 - core) * C + c)
            weight_copy(i, 0).wait()
            weight_copy(i, 1).wait()
            chunk = xs[j].reshape(B * RS, KC)

            @pl.loop(0, FFL // NT)
            def _(n):
                cols = pl.ds(pl.multiple_of(n * NT, NT), NT)
                acc_g[:, cols] += jnp.dot(chunk, wg[j, :, cols], preferred_element_type=F32)
                acc_u[:, cols] += jnp.dot(chunk, wu[j, :, cols], preferred_element_type=F32)

        @pl.loop(0, FFL // NT)
        def _(n):
            cols = pl.ds(pl.multiple_of(n * NT, NT), NT)
            gate = acc_g[:, cols]
            act[:, cols] = (gate / (1.0 + jnp.exp(-gate)) * acc_u[:, cols]).astype(BF16)

        def s_copy(j):
            return remote(ss.at[j], sr.at[j], s_send.at[j], s_recv.at[j], {"blk": sib})

        def u_copy(j, d):
            return remote(sb.at[j, d], ru.at[j, d], l_send.at[j, d], u_recv.at[j, d], {"blk": up})

        def d_copy(j, d):
            return remote(sb.at[j, d], rd.at[j, d], l_send.at[j, d], d_recv.at[j, d], {"blk": down})

        def o_copy(j):
            return remote(fo.at[j], ob.at[sect], o_send.at[j], o_recv.at[sect], {"sect": j})

        def project(i):
            j = order(i)
            p = lax.rem(i, 2)
            weight_copy(i, 2).wait()

            @pl.loop(0, KC // NK)
            def _(n):
                cols = pl.ds(pl.multiple_of(n * NK, NK), NK)
                part = jnp.dot(act[...], wd[j, :, cols], preferred_element_type=F32)
                pf[p, :, :, :, cols] = part.reshape(2, C, RS, NK)

            ss[j] = pf[p, 1 - core].astype(BF16)
            s_copy(j).start()

        def stage(i):
            j = order(i)
            p = lax.rem(i, 2)
            s_copy(j).wait_recv()

            def ups():
                for e in range(C - 1):
                    d = C - 1 - e

                    @pl.when(d > chip)
                    def _():
                        mine = pf[p, core, d] + sr[j, d].astype(F32)

                        @pl.when(has_down)
                        def _():
                            u_copy(j, d).wait_recv()
                            sb[j, d] = (mine + ru[j, d].astype(F32)).astype(BF16)

                        @pl.when(jnp.logical_not(has_down))
                        def _():
                            sb[j, d] = mine.astype(BF16)

                        u_copy(j, d).start()

            def downs():
                for d in range(C - 1):
                    @pl.when(d < chip)
                    def _():
                        mine = pf[p, core, d] + sr[j, d].astype(F32)

                        @pl.when(has_up)
                        def _():
                            d_copy(j, d).wait_recv()
                            sb[j, d] = (mine + rd[j, d].astype(F32)).astype(BF16)

                        @pl.when(jnp.logical_not(has_up))
                        def _():
                            sb[j, d] = mine.astype(BF16)

                        d_copy(j, d).start()

            @pl.when(2 * chip < C)
            def _():
                ups()
                downs()

            @pl.when(2 * chip >= C)
            def _():
                downs()
                ups()

            own[j] = pf[p, core, chip] + sr[j, chip].astype(F32) + rs[j].astype(F32)

        def finish(i):
            j = order(i)

            @pl.when(has_down)
            def _():
                u_copy(j, chip).wait_recv()
                own[j] += ru[j, chip].astype(F32)

            @pl.when(has_up)
            def _():
                d_copy(j, chip).wait_recv()
                own[j] += rd[j, chip].astype(F32)

            @pl.when(i < S - 1)
            def _():
                fo[j] = own[j].astype(BF16)
                o_copy(j).start()

            @pl.when(i == S - 1)
            def _():
                ob[j] = own[j].astype(BF16)

        @pl.loop(0, S + 2)
        def _(i):
            @pl.when(i < S)
            def _():
                project(i)

            @pl.when((i >= 1) & (i <= S))
            def _():
                stage(i - 1)

            @pl.when(i >= 2)
            def _():
                finish(i - 2)

        for i in range(S - 1):
            a_copy(order(i)).wait_send()
            o_copy(order(i)).wait_send()

        @pl.loop(0, S)
        def _(j):
            s_copy(j).wait_send()
            for c in range(C):
                x_sib(j, c).wait_send()

                @pl.when((c <= chip) & has_up)
                def _():
                    x_line(j, c, 0).wait_send()

                @pl.when((c >= chip) & has_down)
                def _():
                    x_line(j, c, 1).wait_send()

                @pl.when(c != chip)
                def _():
                    u_copy(j, c).wait_send()

        for i in range(S - 1):
            t = order(i)
            remote(fo.at[t], ob.at[t], o_send.at[t], o_recv.at[t], {"sect": t}).wait_recv()
        for t in range(S):
            out_ref[t * RS:(t + 1) * RS, :] = ob[t]

    pl.run_scoped(
        middle,
        pltpu.VMEM((B * RS, FFL), F32),
        pltpu.VMEM((B * RS, FFL), F32),
        pltpu.VMEM((B * RS, FFL), BF16),
        pltpu.VMEM((2, 2, C, RS, KC), F32),
    )


def body(S, B, queries, kv_cache, lengths, resid_in, norm_gain, w_gate, w_up, w_down):
    C = B // 2
    rows, KC = queries.shape
    RS = rows // S
    ffl = w_gate.shape[1]
    dma = pltpu.SemaphoreType.DMA
    vmem = pl.BlockSpec(memory_space=pltpu.VMEM)
    hbm = pl.BlockSpec(memory_space=pl.ANY)
    return pl.pallas_call(
        functools.partial(kernel, S, C),
        out_shape=jax.ShapeDtypeStruct((rows, KC), BF16),
        in_specs=[vmem, hbm, vmem, vmem, vmem, hbm, hbm, hbm],
        out_specs=vmem,
        scratch_shapes=[
            pltpu.VMEM((S, KC, ffl), BF16),
            pltpu.VMEM((S, KC, ffl), BF16),
            pltpu.VMEM((S, ffl, KC), BF16),
            pltpu.VMEM((S, RS, KC), BF16),
            pltpu.VMEM((S, RS, KC), BF16),
            pltpu.VMEM((S, B, RS, KC), BF16),
            pltpu.VMEM((S, C, RS, KC), BF16),
            pltpu.VMEM((S, C, RS, KC), BF16),
            pltpu.VMEM((S, C, RS, KC), BF16),
            pltpu.VMEM((S, C, RS, KC), BF16),
            pltpu.VMEM((S, C, RS, KC), BF16),
            pltpu.VMEM((S, RS, KC), F32),
            pltpu.VMEM((S, RS, KC), BF16),
            pltpu.VMEM((S, RS, KC), BF16),
            dma((S,)),
            dma((3, S)),
            dma((S,)),
            dma((S,)),
            dma((S, C, 3)),
            dma((S, B)),
            dma((S,)),
            dma((S,)),
            dma((S, C)),
            dma((S, C)),
            dma((S, C)),
            dma((S,)),
            dma((S,)),
        ],
        compiler_params=pltpu.CompilerParams(
            collective_id=0, has_side_effects=True, vmem_limit_bytes=63 * 1024 * 1024
        ),
    )(
        queries, kv_cache, lengths.reshape(rows, 1), resid_in,
        norm_gain.reshape(S, 1, KC), w_gate, w_up, w_down,
    )


def solution(mesh):
    placed = (
        P("blk", "sect"),
        P("blk", None, "sect"),
        P("blk"),
        P("blk", "sect"),
        P(),
        P(None, "blk"),
        P(None, "blk"),
        P("blk", None),
    )
    return jax.shard_map(
        functools.partial(body, mesh.shape["sect"], mesh.shape["blk"]),
        mesh=mesh, in_specs=placed, out_specs=P("blk", "sect"), check_vma=False,
    )
```

```python
import functools

import jax
import jax.numpy as jnp
from jax import lax
from jax.experimental import pallas as pl
from jax.experimental.pallas import tpu as pltpu
from jax.sharding import PartitionSpec as P

HD = 128
GROUP = 4
TILE = 16
MESH = pl.DeviceIdType.MESH
F32 = jnp.float32
BF16 = jnp.bfloat16


def kernel(
    S, C,
    q_ref, kv_hbm, len_ref, resid_ref, gain_ref, wg_hbm, wu_hbm, wd_hbm,
    out_ref,
    wg, wu, wd, hb, count, xs, ss, sr, sb, ru, rd, own, fo, ob,
    kv_sem, w_sem, a_send, a_recv, x_send, x_recv, s_send, s_recv,
    l_send, u_recv, d_recv, o_send, o_recv,
):
    RS = hb.shape[1]
    KC = hb.shape[2]
    B = 2 * C
    FFL = wg.shape[2]
    heads = kv_hbm.shape[2] // (2 * HD)
    slots = kv_hbm.shape[1]
    NT = 256 if FFL % 256 == 0 else 128
    NK = 256 if KC % 256 == 0 else 128

    sect = lax.axis_index("sect")
    blk = lax.axis_index("blk")
    chip = blk // 2
    core = blk % 2
    sib = chip * 2 + (1 - core)
    up = blk + 2
    down = blk - 2
    has_up = chip < C - 1
    has_down = chip > 0
    me = core * C + chip

    def turn(i):
        return lax.rem(sect + 1 + i, S)

    def order(i):
        return lax.rem(sect + 2 * S - 1 - i, S)

    def remote(src, dst, ssem, rsem, dev):
        return pltpu.make_async_remote_copy(
            src_ref=src, dst_ref=dst, send_sem=ssem, recv_sem=rsem,
            device_id=dev, device_id_type=MESH,
        )

    def weight_copy(i, w):
        t = order(i)
        rows = pl.ds(pl.multiple_of(t * KC, KC), KC)
        src = (wg_hbm.at[rows, :], wu_hbm.at[rows, :], wd_hbm.at[:, rows])[w]
        return pltpu.make_async_copy(src, (wg, wu, wd)[w].at[t], w_sem.at[w, t])

    def greet():
        barrier = pltpu.get_barrier_semaphore()
        for e in range(1, S):
            pl.semaphore_signal(
                barrier, inc=1, device_id={"sect": lax.rem(sect + e, S)}, device_id_type=MESH
            )
        pl.semaphore_signal(barrier, inc=1, device_id={"blk": sib}, device_id_type=MESH)

        @pl.when(has_up)
        def _():
            pl.semaphore_signal(barrier, inc=1, device_id={"blk": up}, device_id_type=MESH)

        @pl.when(has_down)
        def _():
            pl.semaphore_signal(barrier, inc=1, device_id={"blk": down}, device_id_type=MESH)

        pl.semaphore_wait(barrier, S + has_up.astype(jnp.int32) + has_down.astype(jnp.int32))

    def a_copy(t):
        return remote(hb.at[t], xs.at[sect, me], a_send.at[t], a_recv.at[sect], {"sect": t})

    def a_wait(t):
        remote(hb.at[t], xs.at[t, me], a_send.at[t], a_recv.at[t], {"sect": t}).wait_recv()

    def x_line(j, c, which):
        slot = core * C + c
        return remote(
            xs.at[j, slot], xs.at[j, slot], x_send.at[j, c, which], x_recv.at[j, slot],
            {"blk": up if which == 0 else down},
        )

    def x_sib(j, c):
        slot = core * C + c
        return remote(
            xs.at[j, slot], xs.at[j, slot], x_send.at[j, c, 2], x_recv.at[j, slot], {"blk": sib}
        )

    def x_wait(j, slot):
        remote(
            xs.at[j, slot], xs.at[j, slot], x_send.at[j, 0, 0], x_recv.at[j, slot], {"blk": sib}
        ).wait_recv()

    def send_own(j):
        @pl.when(has_up)
        def _():
            x_line(j, chip, 0).start()

        @pl.when(has_down)
        def _():
            x_line(j, chip, 1).start()

        x_sib(j, chip).start()

    def pass_on(i, s):
        j = order(i)

        @pl.when(chip - s >= 0)
        def _():
            x_wait(j, core * C + chip - s)

            @pl.when(has_up)
            def _():
                x_line(j, chip - s, 0).start()

            x_sib(j, chip - s).start()

        @pl.when(chip + s < C)
        def _():
            x_wait(j, core * C + chip + s)

            @pl.when(has_down)
            def _():
                x_line(j, chip + s, 1).start()

            x_sib(j, chip + s).start()

    def pass_due(tick, s):
        @pl.when((tick - s >= 0) & (tick - s < S))
        def _():
            pass_on(tick - s, s)

    def front(kv):
        def kv_copy(t):
            rows = pl.ds(pl.multiple_of(t * RS, RS), RS)
            return pltpu.make_async_copy(kv_hbm.at[rows], kv.at[t], kv_sem.at[t])

        for i in range(S):
            kv_copy(turn(i)).start()
        for i in range(S):
            weight_copy(i, 0).start()
            weight_copy(i, 1).start()
        for i in range(S):
            weight_copy(i, 2).start()

        def attend(t):
            kv_copy(t).wait()
            for g in range(RS // TILE):
                rows = pl.ds(pl.multiple_of(t * RS + g * TILE, TILE), TILE)
                ends = jnp.concatenate([count[rows, 0:1]] * GROUP, axis=0)
                shape = (GROUP * TILE, TILE * slots)
                row = lax.rem(lax.broadcasted_iota(jnp.int32, shape, 0), TILE)
                col = lax.broadcasted_iota(jnp.int32, shape, 1) - row * slots
                live = (col >= 0) & (col < ends)
                for h in range(heads):
                    base = h * GROUP * HD
                    query = jnp.concatenate(
                        [q_ref[rows, base + e * HD:base + (e + 1) * HD] for e in range(GROUP)], axis=0
                    )
                    part = kv[t, g * TILE:(g + 1) * TILE, :, h * 2 * HD:(h + 1) * 2 * HD]
                    part = part.reshape(TILE * slots, 2 * HD)
                    scores = lax.dot_general(
                        query, part[:, :HD], (((1,), (1,)), ((), ())), preferred_element_type=F32
                    ) * (HD ** -0.5)
                    scores = jnp.where(live, scores, -1e30)
                    top = jnp.max(scores, axis=1, keepdims=True)
                    expo = jnp.where(live, jnp.exp(scores - top), 0.0)
                    probs = (expo / jnp.sum(expo, axis=1, keepdims=True)).astype(BF16)
                    attn = jnp.dot(probs, part[:, HD:], preferred_element_type=F32)
                    for e in range(GROUP):
                        cols = slice(base + e * HD, base + (e + 1) * HD)
                        hb[t, g * TILE:(g + 1) * TILE, cols] = (
                            resid_ref[rows, cols].astype(F32) + attn[e * TILE:(e + 1) * TILE]
                        ).astype(BF16)

        rows_all = len_ref.shape[1]
        count[...] = jnp.broadcast_to(len_ref[...], (rows_all, rows_all)).T
        greet()

        @pl.loop(0, S)
        def _(i):
            t = turn(i)
            attend(t)

            @pl.when(i < S - 1)
            def _():
                a_copy(t).start()

            @pl.when(i > 0)
            def _():
                a_wait(order(i - 1))
                send_own(order(i - 1))

            @pl.when(i == S - 1)
            def _():
                xs[t, me] = hb[t]
                send_own(t)

            for s in range(1, C):
                pass_due(i - 1, s)

    pl.run_scoped(front, pltpu.VMEM((S, RS, slots, kv_hbm.shape[2]), BF16))

    def middle(acc_g, acc_u, act, pf, scaled, square):
        acc_g[...] = jnp.zeros_like(acc_g)
        acc_u[...] = jnp.zeros_like(acc_u)
        square[...] = jnp.zeros_like(square)
        for tick in range(S - 1, max(S, C)):
            for s in range(1, C):
                pass_due(tick, s)

        @pl.loop(0, S)
        def _(i):
            j = order(i)
            for c in range(C):
                x_wait(j, (1 - core) * C + c)
            for b in range(B):
                state = xs[j, b].astype(F32)
                rows = slice(b * RS, (b + 1) * RS)
                scaled[rows, :] = (state * gain_ref[j]).astype(BF16)
                state = state * state
                part = state[:, :HD]
                for e in range(1, KC // HD):
                    part = part + state[:, e * HD:(e + 1) * HD]
                square[rows, :] += part
            weight_copy(i, 0).wait()
            weight_copy(i, 1).wait()

            @pl.loop(0, FFL // NT)
            def _(n):
                cols = pl.ds(pl.multiple_of(n * NT, NT), NT)
                acc_g[:, cols] += jnp.dot(scaled[...], wg[j, :, cols], preferred_element_type=F32)
                acc_u[:, cols] += jnp.dot(scaled[...], wu[j, :, cols], preferred_element_type=F32)
                for s in range(1, C):
                    @pl.when(n == min(s, FFL // NT - 1))
                    def _():
                        pass_due(max(S, C) + i, s)

        square[:, 0:1] = lax.rsqrt(
            jnp.sum(square[...], axis=1, keepdims=True) / (S * KC) + 1e-5
        )

        @pl.loop(0, FFL // NT)
        def _(n):
            cols = pl.ds(pl.multiple_of(n * NT, NT), NT)
            inv = square[:, 0:1]
            gate = acc_g[:, cols] * inv
            act[:, cols] = (gate / (1.0 + jnp.exp(-gate)) * (acc_u[:, cols] * inv)).astype(BF16)

        def s_copy(j):
            return remote(ss.at[j], sr.at[j], s_send.at[j], s_recv.at[j], {"blk": sib})

        def u_copy(j, d):
            return remote(sb.at[j, d], ru.at[j, d], l_send.at[j, d], u_recv.at[j, d], {"blk": up})

        def d_copy(j, d):
            return remote(sb.at[j, d], rd.at[j, d], l_send.at[j, d], d_recv.at[j, d], {"blk": down})

        def o_copy(j):
            return remote(fo.at[j], ob.at[sect], o_send.at[j], o_recv.at[sect], {"sect": j})

        def project(i):
            j = order(i)
            p = lax.rem(i, 2)
            weight_copy(i, 2).wait()

            @pl.loop(0, KC // NK)
            def _(n):
                cols = pl.ds(pl.multiple_of(n * NK, NK), NK)
                part = jnp.dot(act[...], wd[j, :, cols], preferred_element_type=F32)
                pf[p, :, :, :, cols] = part.reshape(2, C, RS, NK)

            ss[j] = pf[p, 1 - core].astype(BF16)
            s_copy(j).start()

        def stage(i):
            j = order(i)
            p = lax.rem(i, 2)
            s_copy(j).wait_recv()

            def ups():
                for e in range(C - 1):
                    d = C - 1 - e

                    @pl.when(d > chip)
                    def _():
                        mine = pf[p, core, d] + sr[j, d].astype(F32)

                        @pl.when(has_down)
                        def _():
                            u_copy(j, d).wait_recv()
                            sb[j, d] = (mine + ru[j, d].astype(F32)).astype(BF16)

                        @pl.when(jnp.logical_not(has_down))
                        def _():
                            sb[j, d] = mine.astype(BF16)

                        u_copy(j, d).start()

            def downs():
                for d in range(C - 1):
                    @pl.when(d < chip)
                    def _():
                        mine = pf[p, core, d] + sr[j, d].astype(F32)

                        @pl.when(has_up)
                        def _():
                            d_copy(j, d).wait_recv()
                            sb[j, d] = (mine + rd[j, d].astype(F32)).astype(BF16)

                        @pl.when(jnp.logical_not(has_up))
                        def _():
                            sb[j, d] = mine.astype(BF16)

                        d_copy(j, d).start()

            @pl.when(2 * chip < C)
            def _():
                ups()
                downs()

            @pl.when(2 * chip >= C)
            def _():
                downs()
                ups()

            own[j] = pf[p, core, chip] + sr[j, chip].astype(F32) + xs[j, me].astype(F32)

        def finish(i):
            j = order(i)

            @pl.when(has_down)
            def _():
                u_copy(j, chip).wait_recv()
                own[j] += ru[j, chip].astype(F32)

            @pl.when(has_up)
            def _():
                d_copy(j, chip).wait_recv()
                own[j] += rd[j, chip].astype(F32)

            @pl.when(i < S - 1)
            def _():
                fo[j] = own[j].astype(BF16)
                o_copy(j).start()

            @pl.when(i == S - 1)
            def _():
                ob[j] = own[j].astype(BF16)

        @pl.loop(0, S + 3)
        def _(i):
            @pl.when(i < S)
            def _():
                project(i)

            @pl.when((i >= 1) & (i <= S))
            def _():
                stage(i - 1)

            @pl.when(i >= 3)
            def _():
                finish(i - 3)

        for i in range(S - 1):
            a_copy(turn(i)).wait_send()
            o_copy(order(i)).wait_send()

        @pl.loop(0, S)
        def _(j):
            s_copy(j).wait_send()
            for c in range(C):
                x_sib(j, c).wait_send()

                @pl.when((c <= chip) & has_up)
                def _():
                    x_line(j, c, 0).wait_send()

                @pl.when((c >= chip) & has_down)
                def _():
                    x_line(j, c, 1).wait_send()

                @pl.when(c != chip)
                def _():
                    u_copy(j, c).wait_send()

        for i in range(S - 1):
            t = order(i)
            remote(fo.at[t], ob.at[t], o_send.at[t], o_recv.at[t], {"sect": t}).wait_recv()
        for t in range(S):
            out_ref[t * RS:(t + 1) * RS, :] = ob[t]

    pl.run_scoped(
        middle,
        pltpu.VMEM((B * RS, FFL), F32),
        pltpu.VMEM((B * RS, FFL), F32),
        pltpu.VMEM((B * RS, FFL), BF16),
        pltpu.VMEM((2, 2, C, RS, KC), F32),
        pltpu.VMEM((B * RS, KC), BF16),
        pltpu.VMEM((B * RS, HD), F32),
    )


def body(S, B, queries, kv_cache, lengths, resid_in, norm_gain, w_gate, w_up, w_down):
    C = B // 2
    rows, KC = queries.shape
    RS = rows // S
    ffl = w_gate.shape[1]
    dma = pltpu.SemaphoreType.DMA
    vmem = pl.BlockSpec(memory_space=pltpu.VMEM)
    hbm = pl.BlockSpec(memory_space=pl.ANY)
    return pl.pallas_call(
        functools.partial(kernel, S, C),
        out_shape=jax.ShapeDtypeStruct((rows, KC), BF16),
        in_specs=[vmem, hbm, vmem, vmem, vmem, hbm, hbm, hbm],
        out_specs=vmem,
        scratch_shapes=[
            pltpu.VMEM((S, KC, ffl), BF16),
            pltpu.VMEM((S, KC, ffl), BF16),
            pltpu.VMEM((S, ffl, KC), BF16),
            pltpu.VMEM((S, RS, KC), BF16),
            pltpu.VMEM((rows, rows), jnp.int32),
            pltpu.VMEM((S, B, RS, KC), BF16),
            pltpu.VMEM((S, C, RS, KC), BF16),
            pltpu.VMEM((S, C, RS, KC), BF16),
            pltpu.VMEM((S, C, RS, KC), BF16),
            pltpu.VMEM((S, C, RS, KC), BF16),
            pltpu.VMEM((S, C, RS, KC), BF16),
            pltpu.VMEM((S, RS, KC), F32),
            pltpu.VMEM((S, RS, KC), BF16),
            pltpu.VMEM((S, RS, KC), BF16),
            dma((S,)),
            dma((3, S)),
            dma((S,)),
            dma((S,)),
            dma((S, C, 3)),
            dma((S, B)),
            dma((S,)),
            dma((S,)),
            dma((S, C)),
            dma((S, C)),
            dma((S, C)),
            dma((S,)),
            dma((S,)),
        ],
        compiler_params=pltpu.CompilerParams(
            collective_id=0, has_side_effects=True, vmem_limit_bytes=63 * 1024 * 1024
        ),
    )(
        queries, kv_cache, lengths.reshape(1, rows), resid_in,
        norm_gain.reshape(S, 1, KC), w_gate, w_up, w_down,
    )


def solution(mesh):
    placed = (
        P("blk", "sect"),
        P("blk", None, "sect"),
        P("blk"),
        P("blk", "sect"),
        P(),
        P(None, "blk"),
        P(None, "blk"),
        P("blk", None),
    )
    return jax.shard_map(
        functools.partial(body, mesh.shape["sect"], mesh.shape["blk"]),
        mesh=mesh, in_specs=placed, out_specs=P("blk", "sect"), check_vma=False,
    )
```

```python
import functools

import jax
import jax.numpy as jnp
from jax import lax
from jax.experimental import pallas as pl
from jax.experimental.pallas import tpu as pltpu
from jax.sharding import PartitionSpec as P

HD = 128
GROUP = 4
TILE = 16
MESH = pl.DeviceIdType.MESH
F32 = jnp.float32
BF16 = jnp.bfloat16


def widest(total, most):
    return max(w for w in range(128, most + 1, 128) if total % w == 0)


def kernel(
    S, C,
    q_ref, kv_hbm, len_ref, resid_ref, gain_ref, wg_hbm, wu_hbm, wd_hbm,
    out_ref,
    wg, wu, wd, hb, count, xs, ss, sr, sb, ru, rd, own, fo, ob,
    kv_sem, w_sem, a_send, a_recv, x_send, x_recv, s_send, s_recv,
    l_send, u_recv, d_recv, o_send, o_recv,
):
    RS = hb.shape[1]
    KC = hb.shape[2]
    B = 2 * C
    FFL = wg.shape[2]
    heads = kv_hbm.shape[2] // (2 * HD)
    slots = kv_hbm.shape[1]
    NT = widest(FFL, 1024)
    NK = widest(KC, 512)

    sect = lax.axis_index("sect")
    blk = lax.axis_index("blk")
    chip = blk // 2
    core = blk % 2
    sib = chip * 2 + (1 - core)
    up = blk + 2
    down = blk - 2
    has_up = chip < C - 1
    has_down = chip > 0
    me = core * C + chip

    def turn(i):
        return lax.rem(sect + 1 + i, S)

    def order(i):
        return lax.rem(sect + 2 * S - 1 - i, S)

    def remote(src, dst, ssem, rsem, dev):
        return pltpu.make_async_remote_copy(
            src_ref=src, dst_ref=dst, send_sem=ssem, recv_sem=rsem,
            device_id=dev, device_id_type=MESH,
        )

    def weight_copy(i, w):
        t = order(i)
        rows = pl.ds(pl.multiple_of(t * KC, KC), KC)
        src = (wg_hbm.at[rows, :], wu_hbm.at[rows, :], wd_hbm.at[:, rows])[w]
        return pltpu.make_async_copy(src, (wg, wu, wd)[w].at[t], w_sem.at[w, t])

    def greet():
        barrier = pltpu.get_barrier_semaphore()
        for e in range(1, S):
            pl.semaphore_signal(
                barrier, inc=1, device_id={"sect": lax.rem(sect + e, S)}, device_id_type=MESH
            )
        pl.semaphore_signal(barrier, inc=1, device_id={"blk": sib}, device_id_type=MESH)

        @pl.when(has_up)
        def _():
            pl.semaphore_signal(barrier, inc=1, device_id={"blk": up}, device_id_type=MESH)

        @pl.when(has_down)
        def _():
            pl.semaphore_signal(barrier, inc=1, device_id={"blk": down}, device_id_type=MESH)

        pl.semaphore_wait(barrier, S + has_up.astype(jnp.int32) + has_down.astype(jnp.int32))

    def a_copy(t):
        return remote(hb.at[t], xs.at[sect, me], a_send.at[t], a_recv.at[sect], {"sect": t})

    def a_wait(t):
        remote(hb.at[t], xs.at[t, me], a_send.at[t], a_recv.at[t], {"sect": t}).wait_recv()

    def x_line(j, c, which):
        slot = core * C + c
        return remote(
            xs.at[j, slot], xs.at[j, slot], x_send.at[j, c, which], x_recv.at[j, slot],
            {"blk": up if which == 0 else down},
        )

    def x_sib(j, c):
        slot = core * C + c
        return remote(
            xs.at[j, slot], xs.at[j, slot], x_send.at[j, c, 2], x_recv.at[j, slot], {"blk": sib}
        )

    def x_wait(j, slot):
        remote(
            xs.at[j, slot], xs.at[j, slot], x_send.at[j, 0, 0], x_recv.at[j, slot], {"blk": sib}
        ).wait_recv()

    def send_own(j):
        @pl.when(has_up)
        def _():
            x_line(j, chip, 0).start()

        @pl.when(has_down)
        def _():
            x_line(j, chip, 1).start()

        x_sib(j, chip).start()

    def pass_on(i, s):
        j = order(i)

        @pl.when(chip - s >= 0)
        def _():
            x_wait(j, core * C + chip - s)

            @pl.when(has_up)
            def _():
                x_line(j, chip - s, 0).start()

            x_sib(j, chip - s).start()

        @pl.when(chip + s < C)
        def _():
            x_wait(j, core * C + chip + s)

            @pl.when(has_down)
            def _():
                x_line(j, chip + s, 1).start()

            x_sib(j, chip + s).start()

    def pass_due(tick, s):
        @pl.when((tick - s >= 0) & (tick - s < S))
        def _():
            pass_on(tick - s, s)

    def front(kv):
        def kv_copy(t):
            rows = pl.ds(pl.multiple_of(t * RS, RS), RS)
            return pltpu.make_async_copy(kv_hbm.at[rows], kv.at[t], kv_sem.at[t])

        for i in range(S):
            kv_copy(turn(i)).start()
        def attend(t):
            kv_copy(t).wait()
            for g in range(RS // TILE):
                rows = pl.ds(pl.multiple_of(t * RS + g * TILE, TILE), TILE)
                ends = jnp.concatenate([count[rows, 0:1]] * GROUP, axis=0)
                shape = (GROUP * TILE, TILE * slots)
                row = lax.rem(lax.broadcasted_iota(jnp.int32, shape, 0), TILE)
                col = lax.broadcasted_iota(jnp.int32, shape, 1) - row * slots
                live = (col >= 0) & (col < ends)
                for h in range(heads):
                    base = h * GROUP * HD
                    query = jnp.concatenate(
                        [q_ref[rows, base + e * HD:base + (e + 1) * HD] for e in range(GROUP)], axis=0
                    )
                    part = kv[t, g * TILE:(g + 1) * TILE, :, h * 2 * HD:(h + 1) * 2 * HD]
                    part = part.reshape(TILE * slots, 2 * HD)
                    scores = lax.dot_general(
                        query, part[:, :HD], (((1,), (1,)), ((), ())), preferred_element_type=F32
                    ) * (HD ** -0.5)
                    scores = jnp.where(live, scores, -1e30)
                    top = jnp.max(scores, axis=1, keepdims=True)
                    expo = jnp.where(live, jnp.exp(scores - top), 0.0)
                    probs = (expo * (1.0 / jnp.sum(expo, axis=1, keepdims=True))).astype(BF16)
                    attn = jnp.dot(probs, part[:, HD:], preferred_element_type=F32)
                    for e in range(GROUP):
                        cols = slice(base + e * HD, base + (e + 1) * HD)
                        hb[t, g * TILE:(g + 1) * TILE, cols] = (
                            resid_ref[rows, cols].astype(F32) + attn[e * TILE:(e + 1) * TILE]
                        ).astype(BF16)

        rows_all = len_ref.shape[1]
        count[...] = jnp.broadcast_to(len_ref[...], (rows_all, rows_all)).T
        greet()

        @pl.loop(0, S)
        def _(i):
            t = turn(i)
            attend(t)

            @pl.when(i < S - 1)
            def _():
                a_copy(t).start()

            @pl.when(i < 2)
            def _():
                weight_copy(i, 0).start()
                weight_copy(i, 1).start()

            @pl.when(i > 0)
            def _():
                a_wait(order(i - 1))
                send_own(order(i - 1))

            @pl.when(i == S - 1)
            def _():
                xs[t, me] = hb[t]
                send_own(t)

            for s in range(1, C):
                pass_due(i - 1, s)

    pl.run_scoped(front, pltpu.VMEM((S, RS, slots, kv_hbm.shape[2]), BF16))

    def middle(acc_g, acc_u, act, pf, scaled, square):
        acc_g[...] = jnp.zeros_like(acc_g)
        acc_u[...] = jnp.zeros_like(acc_u)
        square[...] = jnp.zeros_like(square)
        for tick in range(S - 1, max(S, C)):
            for s in range(1, C):
                pass_due(tick, s)

        @pl.loop(0, S)
        def _(i):
            j = order(i)
            for c in range(C):
                x_wait(j, (1 - core) * C + c)
            for b in range(B):
                state = xs[j, b].astype(F32)
                rows = slice(b * RS, (b + 1) * RS)
                scaled[rows, :] = (state * gain_ref[j]).astype(BF16)
                state = state * state
                part = state[:, :HD]
                for e in range(1, KC // HD):
                    part = part + state[:, e * HD:(e + 1) * HD]
                square[rows, :] += part
            weight_copy(i, 0).wait()
            weight_copy(i, 1).wait()

            @pl.when(i + 2 < S)
            def _():
                weight_copy(i + 2, 0).start()
                weight_copy(i + 2, 1).start()

            weight_copy(i, 2).start()

            @pl.loop(0, FFL // NT)
            def _(n):
                cols = pl.ds(pl.multiple_of(n * NT, NT), NT)
                acc_g[:, cols] += jnp.dot(scaled[...], wg[j, :, cols], preferred_element_type=F32)
                acc_u[:, cols] += jnp.dot(scaled[...], wu[j, :, cols], preferred_element_type=F32)
                for s in range(1, C):
                    @pl.when(n == min(s - 1, FFL // NT - 1))
                    def _():
                        pass_due(max(S, C) + i, s)

        square[:, 0:1] = lax.rsqrt(
            jnp.sum(square[...], axis=1, keepdims=True) / (S * KC) + 1e-5
        )

        @pl.loop(0, FFL // NT)
        def _(n):
            cols = pl.ds(pl.multiple_of(n * NT, NT), NT)
            inv = square[:, 0:1]
            gate = acc_g[:, cols] * inv
            act[:, cols] = (gate / (1.0 + jnp.exp(-gate)) * (acc_u[:, cols] * inv)).astype(BF16)

        def s_copy(j):
            return remote(ss.at[j], sr.at[j], s_send.at[j], s_recv.at[j], {"blk": sib})

        def u_copy(j, d):
            return remote(sb.at[j, d], ru.at[j, d], l_send.at[j, d], u_recv.at[j, d], {"blk": up})

        def d_copy(j, d):
            return remote(sb.at[j, d], rd.at[j, d], l_send.at[j, d], d_recv.at[j, d], {"blk": down})

        def o_copy(j):
            return remote(fo.at[j], ob.at[sect], o_send.at[j], o_recv.at[sect], {"sect": j})

        def project(i):
            j = order(i)
            p = lax.rem(i, 2)
            weight_copy(i, 2).wait()

            @pl.loop(0, KC // NK)
            def _(n):
                cols = pl.ds(pl.multiple_of(n * NK, NK), NK)
                part = jnp.dot(act[...], wd[j, :, cols], preferred_element_type=F32)
                pf[p, :, :, :, cols] = part.reshape(2, C, RS, NK)

            ss[j] = pf[p, 1 - core].astype(BF16)
            s_copy(j).start()

        def stage(i):
            j = order(i)
            p = lax.rem(i, 2)
            s_copy(j).wait_recv()

            def ups():
                for e in range(C - 1):
                    d = C - 1 - e

                    @pl.when(d > chip)
                    def _():
                        mine = pf[p, core, d] + sr[j, d].astype(F32)

                        @pl.when(has_down)
                        def _():
                            u_copy(j, d).wait_recv()
                            sb[j, d] = (mine + ru[j, d].astype(F32)).astype(BF16)

                        @pl.when(jnp.logical_not(has_down))
                        def _():
                            sb[j, d] = mine.astype(BF16)

                        u_copy(j, d).start()

            def downs():
                for d in range(C - 1):
                    @pl.when(d < chip)
                    def _():
                        mine = pf[p, core, d] + sr[j, d].astype(F32)

                        @pl.when(has_up)
                        def _():
                            d_copy(j, d).wait_recv()
                            sb[j, d] = (mine + rd[j, d].astype(F32)).astype(BF16)

                        @pl.when(jnp.logical_not(has_up))
                        def _():
                            sb[j, d] = mine.astype(BF16)

                        d_copy(j, d).start()

            @pl.when(2 * chip < C)
            def _():
                ups()
                downs()

            @pl.when(2 * chip >= C)
            def _():
                downs()
                ups()

            own[j] = pf[p, core, chip] + sr[j, chip].astype(F32) + xs[j, me].astype(F32)

        def finish(i):
            j = order(i)

            @pl.when(has_down)
            def _():
                u_copy(j, chip).wait_recv()
                own[j] += ru[j, chip].astype(F32)

            @pl.when(has_up)
            def _():
                d_copy(j, chip).wait_recv()
                own[j] += rd[j, chip].astype(F32)

            @pl.when(i < S - 1)
            def _():
                fo[j] = own[j].astype(BF16)
                o_copy(j).start()

            @pl.when(i == S - 1)
            def _():
                ob[j] = own[j].astype(BF16)

        @pl.loop(0, S + 3)
        def _(i):
            @pl.when(i < S)
            def _():
                project(i)

            @pl.when((i >= 1) & (i <= S))
            def _():
                stage(i - 1)

            @pl.when(i >= 3)
            def _():
                finish(i - 3)

        for i in range(S - 1):
            a_copy(turn(i)).wait_send()
            o_copy(order(i)).wait_send()

        @pl.loop(0, S)
        def _(j):
            s_copy(j).wait_send()
            for c in range(C):
                x_sib(j, c).wait_send()

                @pl.when((c <= chip) & has_up)
                def _():
                    x_line(j, c, 0).wait_send()

                @pl.when((c >= chip) & has_down)
                def _():
                    x_line(j, c, 1).wait_send()

                @pl.when(c != chip)
                def _():
                    u_copy(j, c).wait_send()

        for i in range(S - 1):
            t = order(i)
            remote(fo.at[t], ob.at[t], o_send.at[t], o_recv.at[t], {"sect": t}).wait_recv()
        for t in range(S):
            out_ref[t * RS:(t + 1) * RS, :] = ob[t]

    pl.run_scoped(
        middle,
        pltpu.VMEM((B * RS, FFL), F32),
        pltpu.VMEM((B * RS, FFL), F32),
        pltpu.VMEM((B * RS, FFL), BF16),
        pltpu.VMEM((2, 2, C, RS, KC), F32),
        pltpu.VMEM((B * RS, KC), BF16),
        pltpu.VMEM((B * RS, HD), F32),
    )


def body(S, B, queries, kv_cache, lengths, resid_in, norm_gain, w_gate, w_up, w_down):
    C = B // 2
    rows, KC = queries.shape
    RS = rows // S
    ffl = w_gate.shape[1]
    dma = pltpu.SemaphoreType.DMA
    vmem = pl.BlockSpec(memory_space=pltpu.VMEM)
    hbm = pl.BlockSpec(memory_space=pl.ANY)
    return pl.pallas_call(
        functools.partial(kernel, S, C),
        out_shape=jax.ShapeDtypeStruct((rows, KC), BF16),
        in_specs=[vmem, hbm, vmem, vmem, vmem, hbm, hbm, hbm],
        out_specs=vmem,
        scratch_shapes=[
            pltpu.VMEM((S, KC, ffl), BF16),
            pltpu.VMEM((S, KC, ffl), BF16),
            pltpu.VMEM((S, ffl, KC), BF16),
            pltpu.VMEM((S, RS, KC), BF16),
            pltpu.VMEM((rows, rows), jnp.int32),
            pltpu.VMEM((S, B, RS, KC), BF16),
            pltpu.VMEM((S, C, RS, KC), BF16),
            pltpu.VMEM((S, C, RS, KC), BF16),
            pltpu.VMEM((S, C, RS, KC), BF16),
            pltpu.VMEM((S, C, RS, KC), BF16),
            pltpu.VMEM((S, C, RS, KC), BF16),
            pltpu.VMEM((S, RS, KC), F32),
            pltpu.VMEM((S, RS, KC), BF16),
            pltpu.VMEM((S, RS, KC), BF16),
            dma((S,)),
            dma((3, S)),
            dma((S,)),
            dma((S,)),
            dma((S, C, 3)),
            dma((S, B)),
            dma((S,)),
            dma((S,)),
            dma((S, C)),
            dma((S, C)),
            dma((S, C)),
            dma((S,)),
            dma((S,)),
        ],
        compiler_params=pltpu.CompilerParams(
            collective_id=0, has_side_effects=True, vmem_limit_bytes=63 * 1024 * 1024
        ),
    )(
        queries, kv_cache, lengths.reshape(1, rows), resid_in,
        norm_gain.reshape(S, 1, KC), w_gate, w_up, w_down,
    )


def solution(mesh):
    placed = (
        P("blk", "sect"),
        P("blk", None, "sect"),
        P("blk"),
        P("blk", "sect"),
        P(),
        P(None, "blk"),
        P(None, "blk"),
        P("blk", None),
    )
    return jax.shard_map(
        functools.partial(body, mesh.shape["sect"], mesh.shape["blk"]),
        mesh=mesh, in_specs=placed, out_specs=P("blk", "sect"), check_vma=False,
    )
```

```python
import functools

import jax
import jax.numpy as jnp
from jax import lax
from jax.experimental import pallas as pl
from jax.experimental.pallas import tpu as pltpu
from jax.sharding import PartitionSpec as P

HD = 128
GROUP = 4
TILE = 16
MESH = pl.DeviceIdType.MESH
F32 = jnp.float32
BF16 = jnp.bfloat16


def widest(total, most):
    return max(w for w in range(128, most + 1, 128) if total % w == 0)


def kernel(
    S, C,
    q_ref, kv_hbm, len_ref, resid_ref, gain_ref, wg_hbm, wu_hbm, wd_hbm,
    out_ref,
    wg, wu, wd, hb, count, xs, ss, sr, sb, ru, rd, own, fo, ob,
    kv_sem, w_sem, a_send, a_recv, x_send, x_recv, s_send, s_recv,
    l_send, u_recv, d_recv, o_send, o_recv,
):
    RS = hb.shape[1]
    KC = hb.shape[2]
    B = 2 * C
    RH = xs.shape[2]
    H = RS // RH
    V = H * S
    FFL = wg.shape[2]
    heads = kv_hbm.shape[2] // (2 * HD)
    slots = kv_hbm.shape[1]
    NT = widest(FFL, 1024)
    NK = widest(KC, 512)

    sect = lax.axis_index("sect")
    blk = lax.axis_index("blk")
    chip = blk // 2
    core = blk % 2
    sib = chip * 2 + (1 - core)
    up = blk + 2
    down = blk - 2
    has_up = chip < C - 1
    has_down = chip > 0
    me = core * C + chip

    def turn(i):
        return lax.rem(sect + 1 + i, S)

    def order(i):
        return lax.rem(sect + 2 * S - 1 - i, S)

    def place(v):
        return (v // S) * S + order(lax.rem(v, S))

    def remote(src, dst, ssem, rsem, dev):
        return pltpu.make_async_remote_copy(
            src_ref=src, dst_ref=dst, send_sem=ssem, recv_sem=rsem,
            device_id=dev, device_id_type=MESH,
        )

    def weight_copy(i, w):
        t = order(i)
        rows = pl.ds(pl.multiple_of(t * KC, KC), KC)
        src = (wg_hbm.at[rows, :], wu_hbm.at[rows, :], wd_hbm.at[:, rows])[w]
        return pltpu.make_async_copy(src, (wg, wu, wd)[w].at[t], w_sem.at[w, t])

    def greet():
        barrier = pltpu.get_barrier_semaphore()
        for e in range(1, S):
            pl.semaphore_signal(
                barrier, inc=1, device_id={"sect": lax.rem(sect + e, S)}, device_id_type=MESH
            )
        pl.semaphore_signal(barrier, inc=1, device_id={"blk": sib}, device_id_type=MESH)

        @pl.when(has_up)
        def _():
            pl.semaphore_signal(barrier, inc=1, device_id={"blk": up}, device_id_type=MESH)

        @pl.when(has_down)
        def _():
            pl.semaphore_signal(barrier, inc=1, device_id={"blk": down}, device_id_type=MESH)

        pl.semaphore_wait(barrier, S + has_up.astype(jnp.int32) + has_down.astype(jnp.int32))

    def a_copy(h, t):
        return remote(
            hb.at[t, pl.ds(h * RH, RH)], xs.at[h * S + sect, me],
            a_send.at[h * S + t], a_recv.at[h * S + sect], {"sect": t},
        )

    def a_wait(j):
        remote(xs.at[j, me], xs.at[j, me], a_send.at[0], a_recv.at[j], {"blk": sib}).wait_recv()

    def x_line(j, c, which):
        slot = core * C + c
        return remote(
            xs.at[j, slot], xs.at[j, slot], x_send.at[j, c, which], x_recv.at[j, slot],
            {"blk": up if which == 0 else down},
        )

    def x_sib(j, c):
        slot = core * C + c
        return remote(
            xs.at[j, slot], xs.at[j, slot], x_send.at[j, c, 2], x_recv.at[j, slot], {"blk": sib}
        )

    def x_wait(j, slot):
        remote(
            xs.at[j, slot], xs.at[j, slot], x_send.at[j, 0, 0], x_recv.at[j, slot], {"blk": sib}
        ).wait_recv()

    def send_own(j):
        @pl.when(has_up)
        def _():
            x_line(j, chip, 0).start()

        @pl.when(has_down)
        def _():
            x_line(j, chip, 1).start()

        x_sib(j, chip).start()

    def pass_on(v, s):
        j = place(v)

        @pl.when(chip - s >= 0)
        def _():
            x_wait(j, core * C + chip - s)

            @pl.when(has_up)
            def _():
                x_line(j, chip - s, 0).start()

            x_sib(j, chip - s).start()

        @pl.when(chip + s < C)
        def _():
            x_wait(j, core * C + chip + s)

            @pl.when(has_down)
            def _():
                x_line(j, chip + s, 1).start()

            x_sib(j, chip + s).start()

    def pass_due(tick, s):
        @pl.when((tick - s >= 0) & (tick - s < V))
        def _():
            pass_on(tick - s, s)

    def own_due(tick):
        @pl.when((tick >= 0) & (tick < V))
        def _():
            @pl.when(lax.rem(tick + S, S) < S - 1)
            def _():
                a_wait(place(tick))

            send_own(place(tick))

    def front(kv):
        def kv_copy(t):
            rows = pl.ds(pl.multiple_of(t * RS, RS), RS)
            return pltpu.make_async_copy(kv_hbm.at[rows], kv.at[t], kv_sem.at[t])

        for i in range(S):
            kv_copy(turn(i)).start()
        def attend(t):
            kv_copy(t).wait()
            for g in range(RS // TILE):
                rows = pl.ds(pl.multiple_of(t * RS + g * TILE, TILE), TILE)
                ends = jnp.concatenate([count[rows, 0:1]] * GROUP, axis=0)
                shape = (GROUP * TILE, TILE * slots)
                row = lax.rem(lax.broadcasted_iota(jnp.int32, shape, 0), TILE)
                col = lax.broadcasted_iota(jnp.int32, shape, 1) - row * slots
                live = (col >= 0) & (col < ends)
                for h in range(heads):
                    base = h * GROUP * HD
                    query = jnp.concatenate(
                        [q_ref[rows, base + e * HD:base + (e + 1) * HD] for e in range(GROUP)], axis=0
                    )
                    part = kv[t, g * TILE:(g + 1) * TILE, :, h * 2 * HD:(h + 1) * 2 * HD]
                    part = part.reshape(TILE * slots, 2 * HD)
                    scores = lax.dot_general(
                        query, part[:, :HD], (((1,), (1,)), ((), ())), preferred_element_type=F32
                    ) * (HD ** -0.5)
                    scores = jnp.where(live, scores, -1e30)
                    top = jnp.max(scores, axis=1, keepdims=True)
                    expo = jnp.where(live, jnp.exp(scores - top), 0.0)
                    probs = (expo * (1.0 / jnp.sum(expo, axis=1, keepdims=True))).astype(BF16)
                    attn = jnp.dot(probs, part[:, HD:], preferred_element_type=F32)
                    for e in range(GROUP):
                        cols = slice(base + e * HD, base + (e + 1) * HD)
                        hb[t, g * TILE:(g + 1) * TILE, cols] = (
                            resid_ref[rows, cols].astype(F32) + attn[e * TILE:(e + 1) * TILE]
                        ).astype(BF16)

        rows_all = len_ref.shape[1]
        count[...] = jnp.broadcast_to(len_ref[...], (rows_all, rows_all)).T
        greet()

        @pl.loop(0, S)
        def _(i):
            t = turn(i)
            attend(t)

            @pl.when(i < S - 1)
            def _():
                for h in range(H):
                    a_copy(h, t).start()

            @pl.when(i < 2)
            def _():
                weight_copy(i, 0).start()
                weight_copy(i, 1).start()

            @pl.when(i == S - 1)
            def _():
                for h in range(H):
                    xs[h * S + t, me] = hb[t, h * RH:(h + 1) * RH]

            own_due(i - 1)
            for s in range(1, C):
                pass_due(i - 1, s)

    pl.run_scoped(front, pltpu.VMEM((S, RS, slots, kv_hbm.shape[2]), BF16))

    def middle(acc_g, acc_u, act, pf, scaled, square):
        for tick in range(S - 1, max(S, C)):
            own_due(tick)
            for s in range(1, C):
                pass_due(tick, s)

        def expand(v):
            i = lax.rem(v, S)
            t = order(i)
            j = place(v)

            @pl.when(i == 0)
            def _():
                acc_g[...] = jnp.zeros_like(acc_g)
                acc_u[...] = jnp.zeros_like(acc_u)
                square[...] = jnp.zeros_like(square)

            own_due(max(S, C) + v)
            for c in range(C):
                x_wait(j, (1 - core) * C + c)
            for b in range(B):
                state = xs[j, b].astype(F32)
                rows = slice(b * RH, (b + 1) * RH)
                scaled[rows, :] = (state * gain_ref[t]).astype(BF16)
                state = state * state
                part = state[:, :HD]
                for e in range(1, KC // HD):
                    part = part + state[:, e * HD:(e + 1) * HD]
                square[rows, :] += part

            @pl.when(v < S)
            def _():
                weight_copy(i, 0).wait()
                weight_copy(i, 1).wait()

                @pl.when(i + 2 < S)
                def _():
                    weight_copy(i + 2, 0).start()
                    weight_copy(i + 2, 1).start()

                weight_copy(i, 2).start()

            @pl.loop(0, FFL // NT)
            def _(n):
                cols = pl.ds(pl.multiple_of(n * NT, NT), NT)
                acc_g[:, cols] += jnp.dot(scaled[...], wg[t, :, cols], preferred_element_type=F32)
                acc_u[:, cols] += jnp.dot(scaled[...], wu[t, :, cols], preferred_element_type=F32)
                for s in range(1, C):
                    @pl.when(n == min(s - 1, FFL // NT - 1))
                    def _():
                        pass_due(max(S, C) + v, s)

        def activate():
            square[:, 0:1] = lax.rsqrt(
                jnp.sum(square[...], axis=1, keepdims=True) / (S * KC) + 1e-5
            )

            @pl.loop(0, FFL // 128)
            def _(n):
                cols = pl.ds(pl.multiple_of(n * 128, 128), 128)
                inv = square[:, 0:1]
                gate = acc_g[:, cols] * inv
                act[:, cols] = (gate / (1.0 + jnp.exp(-gate)) * (acc_u[:, cols] * inv)).astype(BF16)

        @pl.loop(0, S)
        def _(v):
            expand(v)

        activate()

        def s_copy(j):
            return remote(ss.at[j], sr.at[j], s_send.at[j], s_recv.at[j], {"blk": sib})

        def u_copy(j, d):
            return remote(sb.at[j, d], ru.at[j, d], l_send.at[j, d], u_recv.at[j, d], {"blk": up})

        def d_copy(j, d):
            return remote(sb.at[j, d], rd.at[j, d], l_send.at[j, d], d_recv.at[j, d], {"blk": down})

        def o_copy(j):
            there = (j // S) * S + sect
            return remote(
                fo.at[j], ob.at[there], o_send.at[j], o_recv.at[there], {"sect": lax.rem(j, S)}
            )

        def project(v):
            j = place(v)
            t = lax.rem(j, S)
            p = lax.rem(v, 2)

            @pl.when(v < S)
            def _():
                weight_copy(v, 2).wait()

            @pl.loop(0, KC // NK)
            def _(n):
                cols = pl.ds(pl.multiple_of(n * NK, NK), NK)
                part = jnp.dot(act[...], wd[t, :, cols], preferred_element_type=F32)
                pf[p, :, :, :, cols] = part.reshape(2, C, RH, NK)

            ss[j] = pf[p, 1 - core].astype(BF16)
            s_copy(j).start()

        def stage(v):
            j = place(v)
            p = lax.rem(v, 2)
            s_copy(j).wait_recv()

            def ups():
                for e in range(C - 1):
                    d = C - 1 - e

                    @pl.when(d > chip)
                    def _():
                        mine = pf[p, core, d] + sr[j, d].astype(F32)

                        @pl.when(has_down)
                        def _():
                            u_copy(j, d).wait_recv()
                            sb[j, d] = (mine + ru[j, d].astype(F32)).astype(BF16)

                        @pl.when(jnp.logical_not(has_down))
                        def _():
                            sb[j, d] = mine.astype(BF16)

                        u_copy(j, d).start()

            def downs():
                for d in range(C - 1):
                    @pl.when(d < chip)
                    def _():
                        mine = pf[p, core, d] + sr[j, d].astype(F32)

                        @pl.when(has_up)
                        def _():
                            d_copy(j, d).wait_recv()
                            sb[j, d] = (mine + rd[j, d].astype(F32)).astype(BF16)

                        @pl.when(jnp.logical_not(has_up))
                        def _():
                            sb[j, d] = mine.astype(BF16)

                        d_copy(j, d).start()

            @pl.when(2 * chip < C)
            def _():
                ups()
                downs()

            @pl.when(2 * chip >= C)
            def _():
                downs()
                ups()

            own[j] = pf[p, core, chip] + sr[j, chip].astype(F32) + xs[j, me].astype(F32)

        def finish(v):
            j = place(v)
            i = lax.rem(v, S)

            @pl.when(has_down)
            def _():
                u_copy(j, chip).wait_recv()
                own[j] += ru[j, chip].astype(F32)

            @pl.when(has_up)
            def _():
                d_copy(j, chip).wait_recv()
                own[j] += rd[j, chip].astype(F32)

            @pl.when(i < S - 1)
            def _():
                fo[j] = own[j].astype(BF16)
                o_copy(j).start()

            @pl.when(i == S - 1)
            def _():
                ob[j] = own[j].astype(BF16)

        @pl.loop(0, V + 3)
        def _(v):
            if H > 1:
                @pl.when((v > 0) & (v < V) & (lax.rem(v, S) == 0))
                def _():
                    activate()

            @pl.when(v < V)
            def _():
                project(v)

            @pl.when((v >= 1) & (v <= V))
            def _():
                stage(v - 1)

            @pl.when(v >= 3)
            def _():
                finish(v - 3)

            if H > 1:
                @pl.when(v + S < V)
                def _():
                    expand(v + S)

        for h in range(H):
            for i in range(S - 1):
                a_copy(h, turn(i)).wait_send()
                o_copy(h * S + order(i)).wait_send()

        @pl.loop(0, V)
        def _(j):
            s_copy(j).wait_send()
            for c in range(C):
                x_sib(j, c).wait_send()

                @pl.when((c <= chip) & has_up)
                def _():
                    x_line(j, c, 0).wait_send()

                @pl.when((c >= chip) & has_down)
                def _():
                    x_line(j, c, 1).wait_send()

                @pl.when(c != chip)
                def _():
                    u_copy(j, c).wait_send()

        for h in range(H):
            for i in range(S - 1):
                j = h * S + order(i)
                remote(
                    fo.at[j], ob.at[j], o_send.at[j], o_recv.at[j], {"sect": order(i)}
                ).wait_recv()
        for t in range(S):
            for h in range(H):
                out_ref[t * RS + h * RH:t * RS + (h + 1) * RH, :] = ob[h * S + t]

    pl.run_scoped(
        middle,
        pltpu.VMEM((B * RH, FFL), F32),
        pltpu.VMEM((B * RH, FFL), F32),
        pltpu.VMEM((B * RH, FFL), BF16),
        pltpu.VMEM((2, 2, C, RH, KC), F32),
        pltpu.VMEM((B * RH, KC), BF16),
        pltpu.VMEM((B * RH, HD), F32),
    )


def body(S, B, queries, kv_cache, lengths, resid_in, norm_gain, w_gate, w_up, w_down):
    C = B // 2
    rows, KC = queries.shape
    RS = rows // S
    H = 2 if RS % (2 * TILE) == 0 else 1
    RH = RS // H
    V = H * S
    ffl = w_gate.shape[1]
    dma = pltpu.SemaphoreType.DMA
    vmem = pl.BlockSpec(memory_space=pltpu.VMEM)
    hbm = pl.BlockSpec(memory_space=pl.ANY)
    return pl.pallas_call(
        functools.partial(kernel, S, C),
        out_shape=jax.ShapeDtypeStruct((rows, KC), BF16),
        in_specs=[vmem, hbm, vmem, vmem, vmem, hbm, hbm, hbm],
        out_specs=vmem,
        scratch_shapes=[
            pltpu.VMEM((S, KC, ffl), BF16),
            pltpu.VMEM((S, KC, ffl), BF16),
            pltpu.VMEM((S, ffl, KC), BF16),
            pltpu.VMEM((S, RS, KC), BF16),
            pltpu.VMEM((rows, rows), jnp.int32),
            pltpu.VMEM((V, B, RH, KC), BF16),
            pltpu.VMEM((V, C, RH, KC), BF16),
            pltpu.VMEM((V, C, RH, KC), BF16),
            pltpu.VMEM((V, C, RH, KC), BF16),
            pltpu.VMEM((V, C, RH, KC), BF16),
            pltpu.VMEM((V, C, RH, KC), BF16),
            pltpu.VMEM((V, RH, KC), F32),
            pltpu.VMEM((V, RH, KC), BF16),
            pltpu.VMEM((V, RH, KC), BF16),
            dma((S,)),
            dma((3, S)),
            dma((V,)),
            dma((V,)),
            dma((V, C, 3)),
            dma((V, B)),
            dma((V,)),
            dma((V,)),
            dma((V, C)),
            dma((V, C)),
            dma((V, C)),
            dma((V,)),
            dma((V,)),
        ],
        compiler_params=pltpu.CompilerParams(
            collective_id=0, has_side_effects=True, vmem_limit_bytes=63 * 1024 * 1024
        ),
    )(
        queries, kv_cache, lengths.reshape(1, rows), resid_in,
        norm_gain.reshape(S, 1, KC), w_gate, w_up, w_down,
    )


def solution(mesh):
    placed = (
        P("blk", "sect"),
        P("blk", None, "sect"),
        P("blk"),
        P("blk", "sect"),
        P(),
        P(None, "blk"),
        P(None, "blk"),
        P("blk", None),
    )
    return jax.shard_map(
        functools.partial(body, mesh.shape["sect"], mesh.shape["blk"]),
        mesh=mesh, in_specs=placed, out_specs=P("blk", "sect"), check_vma=False,
    )
```

```python
import functools

import jax
import jax.numpy as jnp
from jax import lax
from jax.experimental import pallas as pl
from jax.experimental.pallas import tpu as pltpu
from jax.sharding import PartitionSpec as P

HD = 128
GROUP = 4
TILE = 16
MESH = pl.DeviceIdType.MESH
F32 = jnp.float32
BF16 = jnp.bfloat16


def widest(total, most):
    return max(w for w in range(128, most + 1, 128) if total % w == 0)


def kernel(
    S, C,
    q_ref, kv_hbm, len_ref, resid_ref, gain_ref, wg_hbm, wu_hbm, wd_hbm,
    out_ref,
    wg, wu, wd, hb, count, xs, ss, sr, sb, ru, own, fo, ob,
    kv_sem, w_sem, a_send, a_recv, x_send, x_recv, s_send, s_recv,
    l_send, u_recv, o_send, o_recv,
):
    RS = hb.shape[1]
    KC = hb.shape[2]
    B = 2 * C
    FFL = wg.shape[2]
    heads = kv_hbm.shape[2] // (2 * HD)
    slots = kv_hbm.shape[1]
    NT = widest(FFL, 1024)
    NK = widest(KC, 512)

    sect = lax.axis_index("sect")
    blk = lax.axis_index("blk")
    chip = blk // 2
    core = blk % 2
    sib = chip * 2 + (1 - core)
    up = blk + 2
    down = blk - 2
    has_up = chip < C - 1
    has_down = chip > 0
    me = core * C + chip

    def turn(i):
        return lax.rem(sect + 1 + i, S)

    def order(i):
        return lax.rem(sect + 2 * S - 1 - i, S)

    def remote(src, dst, ssem, rsem, dev):
        return pltpu.make_async_remote_copy(
            src_ref=src, dst_ref=dst, send_sem=ssem, recv_sem=rsem,
            device_id=dev, device_id_type=MESH,
        )

    def weight_copy(i, w):
        t = order(i)
        rows = pl.ds(pl.multiple_of(t * KC, KC), KC)
        src = (wg_hbm.at[rows, :], wu_hbm.at[rows, :], wd_hbm.at[:, rows])[w]
        return pltpu.make_async_copy(src, (wg, wu, wd)[w].at[t], w_sem.at[w, t])

    def greet():
        barrier = pltpu.get_barrier_semaphore()
        for e in range(1, S):
            pl.semaphore_signal(
                barrier, inc=1, device_id={"sect": lax.rem(sect + e, S)}, device_id_type=MESH
            )
        pl.semaphore_signal(barrier, inc=1, device_id={"blk": sib}, device_id_type=MESH)

        for e in range(1, C):
            pl.semaphore_signal(
                barrier, inc=1, device_id={"blk": lax.rem(chip + e, C) * 2 + core},
                device_id_type=MESH,
            )
        pl.semaphore_wait(barrier, S + C - 1)

    def a_copy(t):
        return remote(hb.at[t], xs.at[sect, me], a_send.at[t], a_recv.at[sect], {"sect": t})

    def a_wait(t):
        remote(hb.at[t], xs.at[t, me], a_send.at[t], a_recv.at[t], {"sect": t}).wait_recv()

    def x_line(j, c, which):
        slot = core * C + c
        return remote(
            xs.at[j, slot], xs.at[j, slot], x_send.at[j, c, which], x_recv.at[j, slot],
            {"blk": up if which == 0 else down},
        )

    def x_sib(j, c):
        slot = core * C + c
        return remote(
            xs.at[j, slot], xs.at[j, slot], x_send.at[j, c, 2], x_recv.at[j, slot], {"blk": sib}
        )

    def x_wait(j, slot):
        remote(
            xs.at[j, slot], xs.at[j, slot], x_send.at[j, 0, 0], x_recv.at[j, slot], {"blk": sib}
        ).wait_recv()

    def send_own(j):
        @pl.when(has_up)
        def _():
            x_line(j, chip, 0).start()

        @pl.when(has_down)
        def _():
            x_line(j, chip, 1).start()

        x_sib(j, chip).start()

    def pass_on(i, s):
        j = order(i)

        @pl.when(chip - s >= 0)
        def _():
            x_wait(j, core * C + chip - s)

            @pl.when(has_up)
            def _():
                x_line(j, chip - s, 0).start()

            x_sib(j, chip - s).start()

        @pl.when(chip + s < C)
        def _():
            x_wait(j, core * C + chip + s)

            @pl.when(has_down)
            def _():
                x_line(j, chip + s, 1).start()

            x_sib(j, chip + s).start()

    def pass_due(tick, s):
        @pl.when((tick - s >= 0) & (tick - s < S))
        def _():
            pass_on(tick - s, s)

    def front(kv):
        def kv_copy(t):
            rows = pl.ds(pl.multiple_of(t * RS, RS), RS)
            return pltpu.make_async_copy(kv_hbm.at[rows], kv.at[t], kv_sem.at[t])

        for i in range(S):
            kv_copy(turn(i)).start()
        def attend(t):
            kv_copy(t).wait()
            for g in range(RS // TILE):
                rows = pl.ds(pl.multiple_of(t * RS + g * TILE, TILE), TILE)
                ends = jnp.concatenate([count[rows, 0:1]] * GROUP, axis=0)
                shape = (GROUP * TILE, TILE * slots)
                row = lax.rem(lax.broadcasted_iota(jnp.int32, shape, 0), TILE)
                col = lax.broadcasted_iota(jnp.int32, shape, 1) - row * slots
                live = (col >= 0) & (col < ends)
                for h in range(heads):
                    base = h * GROUP * HD
                    query = jnp.concatenate(
                        [q_ref[rows, base + e * HD:base + (e + 1) * HD] for e in range(GROUP)], axis=0
                    )
                    part = kv[t, g * TILE:(g + 1) * TILE, :, h * 2 * HD:(h + 1) * 2 * HD]
                    part = part.reshape(TILE * slots, 2 * HD)
                    scores = lax.dot_general(
                        query, part[:, :HD], (((1,), (1,)), ((), ())), preferred_element_type=F32
                    ) * (HD ** -0.5)
                    scores = jnp.where(live, scores, -1e30)
                    top = jnp.max(scores, axis=1, keepdims=True)
                    expo = jnp.where(live, jnp.exp(scores - top), 0.0)
                    probs = (expo * (1.0 / jnp.sum(expo, axis=1, keepdims=True))).astype(BF16)
                    attn = jnp.dot(probs, part[:, HD:], preferred_element_type=F32)
                    for e in range(GROUP):
                        cols = slice(base + e * HD, base + (e + 1) * HD)
                        hb[t, g * TILE:(g + 1) * TILE, cols] = (
                            resid_ref[rows, cols].astype(F32) + attn[e * TILE:(e + 1) * TILE]
                        ).astype(BF16)

        rows_all = len_ref.shape[1]
        count[...] = jnp.broadcast_to(len_ref[...], (rows_all, rows_all)).T
        greet()

        @pl.loop(0, S)
        def _(i):
            t = turn(i)
            attend(t)

            @pl.when(i < S - 1)
            def _():
                a_copy(t).start()

            @pl.when(i < 2)
            def _():
                weight_copy(i, 0).start()
                weight_copy(i, 1).start()

            @pl.when(i > 0)
            def _():
                a_wait(order(i - 1))
                send_own(order(i - 1))

            @pl.when(i == S - 1)
            def _():
                xs[t, me] = hb[t]
                send_own(t)

            for s in range(1, C):
                pass_due(i - 1, s)

    pl.run_scoped(front, pltpu.VMEM((S, RS, slots, kv_hbm.shape[2]), BF16))

    def middle(acc_g, acc_u, act, pf, scaled, square):
        acc_g[...] = jnp.zeros_like(acc_g)
        acc_u[...] = jnp.zeros_like(acc_u)
        square[...] = jnp.zeros_like(square)
        for tick in range(S - 1, max(S, C)):
            for s in range(1, C):
                pass_due(tick, s)

        @pl.loop(0, S)
        def _(i):
            j = order(i)
            for c in range(C):
                x_wait(j, (1 - core) * C + c)
            for b in range(B):
                state = xs[j, b].astype(F32)
                rows = slice(b * RS, (b + 1) * RS)
                scaled[rows, :] = (state * gain_ref[j]).astype(BF16)
                state = state * state
                part = state[:, :HD]
                for e in range(1, KC // HD):
                    part = part + state[:, e * HD:(e + 1) * HD]
                square[rows, :] += part
            weight_copy(i, 0).wait()
            weight_copy(i, 1).wait()

            @pl.when(i + 2 < S)
            def _():
                weight_copy(i + 2, 0).start()
                weight_copy(i + 2, 1).start()

            weight_copy(i, 2).start()

            @pl.loop(0, FFL // NT)
            def _(n):
                cols = pl.ds(pl.multiple_of(n * NT, NT), NT)
                acc_g[:, cols] += jnp.dot(scaled[...], wg[j, :, cols], preferred_element_type=F32)
                acc_u[:, cols] += jnp.dot(scaled[...], wu[j, :, cols], preferred_element_type=F32)
                for s in range(1, C):
                    @pl.when(n == min(s - 1, FFL // NT - 1))
                    def _():
                        pass_due(max(S, C) + i, s)

        square[:, 0:1] = lax.rsqrt(
            jnp.sum(square[...], axis=1, keepdims=True) / (S * KC) + 1e-5
        )

        @pl.loop(0, FFL // NT)
        def _(n):
            cols = pl.ds(pl.multiple_of(n * NT, NT), NT)
            inv = square[:, 0:1]
            gate = acc_g[:, cols] * inv
            act[:, cols] = (gate / (1.0 + jnp.exp(-gate)) * (acc_u[:, cols] * inv)).astype(BF16)

        def s_copy(j):
            return remote(ss.at[j], sr.at[j], s_send.at[j], s_recv.at[j], {"blk": sib})

        def r_copy(j, d):
            return remote(
                sb.at[j, d], ru.at[j, chip], l_send.at[j, d], u_recv.at[j, chip],
                {"blk": d * 2 + core},
            )

        def r_wait(j, c):
            remote(
                sb.at[j, c], ru.at[j, c], l_send.at[j, c], u_recv.at[j, c], {"blk": sib}
            ).wait_recv()

        def o_copy(j):
            return remote(fo.at[j], ob.at[sect], o_send.at[j], o_recv.at[sect], {"sect": j})

        def project(i):
            j = order(i)
            p = lax.rem(i, 2)
            weight_copy(i, 2).wait()

            @pl.loop(0, KC // NK)
            def _(n):
                cols = pl.ds(pl.multiple_of(n * NK, NK), NK)
                part = jnp.dot(act[...], wd[j, :, cols], preferred_element_type=F32)
                pf[p, :, :, :, cols] = part.reshape(2, C, RS, NK)

            ss[j] = pf[p, 1 - core].astype(BF16)
            s_copy(j).start()

        def stage(i):
            j = order(i)
            p = lax.rem(i, 2)
            s_copy(j).wait_recv()

            for e in range(C - 1, 0, -1):
                for d in (chip + e, chip - e):
                    @pl.when((d >= 0) & (d < C))
                    def _():
                        sb[j, d] = (pf[p, core, d] + sr[j, d].astype(F32)).astype(BF16)
                        r_copy(j, d).start()

            own[j] = pf[p, core, chip] + sr[j, chip].astype(F32) + xs[j, me].astype(F32)

        def finish(i):
            j = order(i)

            for e in range(1, C):
                c = lax.rem(chip + e, C)
                r_wait(j, c)
                own[j] += ru[j, c].astype(F32)

            @pl.when(i < S - 1)
            def _():
                fo[j] = own[j].astype(BF16)
                o_copy(j).start()

            @pl.when(i == S - 1)
            def _():
                ob[j] = own[j].astype(BF16)

        @pl.loop(0, S + 3)
        def _(i):
            @pl.when(i < S)
            def _():
                project(i)

            @pl.when((i >= 1) & (i <= S))
            def _():
                stage(i - 1)

            @pl.when(i >= 3)
            def _():
                finish(i - 3)

        for i in range(S - 1):
            a_copy(turn(i)).wait_send()
            o_copy(order(i)).wait_send()

        @pl.loop(0, S)
        def _(j):
            s_copy(j).wait_send()
            for c in range(C):
                x_sib(j, c).wait_send()

                @pl.when((c <= chip) & has_up)
                def _():
                    x_line(j, c, 0).wait_send()

                @pl.when((c >= chip) & has_down)
                def _():
                    x_line(j, c, 1).wait_send()

                @pl.when(c != chip)
                def _():
                    r_copy(j, c).wait_send()

        for i in range(S - 1):
            t = order(i)
            remote(fo.at[t], ob.at[t], o_send.at[t], o_recv.at[t], {"sect": t}).wait_recv()
        for t in range(S):
            out_ref[t * RS:(t + 1) * RS, :] = ob[t]

    pl.run_scoped(
        middle,
        pltpu.VMEM((B * RS, FFL), F32),
        pltpu.VMEM((B * RS, FFL), F32),
        pltpu.VMEM((B * RS, FFL), BF16),
        pltpu.VMEM((2, 2, C, RS, KC), F32),
        pltpu.VMEM((B * RS, KC), BF16),
        pltpu.VMEM((B * RS, HD), F32),
    )


def body(S, B, queries, kv_cache, lengths, resid_in, norm_gain, w_gate, w_up, w_down):
    C = B // 2
    rows, KC = queries.shape
    RS = rows // S
    ffl = w_gate.shape[1]
    dma = pltpu.SemaphoreType.DMA
    vmem = pl.BlockSpec(memory_space=pltpu.VMEM)
    hbm = pl.BlockSpec(memory_space=pl.ANY)
    return pl.pallas_call(
        functools.partial(kernel, S, C),
        out_shape=jax.ShapeDtypeStruct((rows, KC), BF16),
        in_specs=[vmem, hbm, vmem, vmem, vmem, hbm, hbm, hbm],
        out_specs=vmem,
        scratch_shapes=[
            pltpu.VMEM((S, KC, ffl), BF16),
            pltpu.VMEM((S, KC, ffl), BF16),
            pltpu.VMEM((S, ffl, KC), BF16),
            pltpu.VMEM((S, RS, KC), BF16),
            pltpu.VMEM((rows, rows), jnp.int32),
            pltpu.VMEM((S, B, RS, KC), BF16),
            pltpu.VMEM((S, C, RS, KC), BF16),
            pltpu.VMEM((S, C, RS, KC), BF16),
            pltpu.VMEM((S, C, RS, KC), BF16),
            pltpu.VMEM((S, C, RS, KC), BF16),
            pltpu.VMEM((S, RS, KC), F32),
            pltpu.VMEM((S, RS, KC), BF16),
            pltpu.VMEM((S, RS, KC), BF16),
            dma((S,)),
            dma((3, S)),
            dma((S,)),
            dma((S,)),
            dma((S, C, 3)),
            dma((S, B)),
            dma((S,)),
            dma((S,)),
            dma((S, C)),
            dma((S, C)),
            dma((S,)),
            dma((S,)),
        ],
        compiler_params=pltpu.CompilerParams(
            collective_id=0, has_side_effects=True, vmem_limit_bytes=63 * 1024 * 1024
        ),
    )(
        queries, kv_cache, lengths.reshape(1, rows), resid_in,
        norm_gain.reshape(S, 1, KC), w_gate, w_up, w_down,
    )


def solution(mesh):
    placed = (
        P("blk", "sect"),
        P("blk", None, "sect"),
        P("blk"),
        P("blk", "sect"),
        P(),
        P(None, "blk"),
        P(None, "blk"),
        P("blk", None),
    )
    return jax.shard_map(
        functools.partial(body, mesh.shape["sect"], mesh.shape["blk"]),
        mesh=mesh, in_specs=placed, out_specs=P("blk", "sect"), check_vma=False,
    )
```
